32 devices in a mesh: pair: 4 (over y, x), slab: 8 (over z, core).
Axes of the slice: x: 2, y: 2, z: 4, core: 2. Of those that a mesh axis runs over, the one named last changes fastest.
Arguments:
- pair_density: bfloat16 [12288, 49152], P('pair', 'slab'), may hold values from -6 to 6
- subspace: bfloat16 [49152, 512], P('slab'), may hold values from -0.02734375 to 0.02734375
- band_valence: int32 [12288], P('pair'), may hold values from 0 to 510, as said below
- band_conduction: int32 [12288], P('pair'), may hold values from 1 to 511, as said below
- occupied: int32 [512], replicated, may hold values from 0 to 1, as said below
- energies: float32 [512], replicated, may hold values from -1 to 1
Outputs:
- chi_panel: float32 [512, 49152], P('pair', 'slab')
- subspace_chi: float32 [512, 512], P('slab', 'pair')
The draws below stay inside these ranges and needn't reach their ends.
Inputs may be any that keep to these rules, and one draw needn't show every extreme that they name: Exactly half of the 512 bands are occupied. `band_valence`: every entry names a band that occupied marks as occupied. `band_conduction`: every entry names a band that occupied marks as unoccupied.
All inputs are finite; a program needn't handle non-finite values.
Results may differ from the reference program's by a relative error of at most 0.0024.
Values sent between devices are 32-bit elements; how exact they have to be, the bound alone decides.
No kernel may reach another device: no remote copies, remote signals or barrier semaphores. Data moves between devices by JAX's collectives and lax.ppermute only.
A program may use at most 128 MiB of HBM per device.

```python
import math
import jax
import jax.numpy as jnp
from jax import lax

G = 49152
NB = 512
NBANDS = 512
PAIRS = 12288


def band_sets(key):
    half = NBANDS // 2
    shuffled = jax.random.permutation(jax.random.fold_in(key, 17), NBANDS - 4).astype(jnp.int32) + 2
    filled_list = jnp.concatenate([jnp.array([0, NBANDS - 2], dtype=jnp.int32), shuffled[:half - 2]])
    empty_list = jnp.concatenate([jnp.array([NBANDS - 1, 1], dtype=jnp.int32), shuffled[half - 2:]])
    occupied = jnp.zeros((NBANDS,), jnp.int32).at[filled_list].set(1)
    low_pick = jax.random.randint(jax.random.fold_in(key, 29), (PAIRS,), 0, half)
    high_pick = jax.random.randint(jax.random.fold_in(key, 41), (PAIRS,), 0, half)
    valence = filled_list[low_pick].at[0].set(0).at[1].set(NBANDS - 2)
    conduction = empty_list[high_pick].at[0].set(NBANDS - 1).at[1].set(1)
    return (valence.astype(jnp.int32), conduction.astype(jnp.int32), occupied)


def draw_band_valence(key, part):
    return band_sets(key)[0]


def draw_band_conduction(key, part):
    return band_sets(key)[1]


def draw_occupied(key, part):
    return band_sets(key)[2]


def block_levels(own_key, extent, shards, smallest, top_value):
    factor_of = 1.0
    for axis_at, shards_of in shards:
        draws = jax.random.uniform(jax.random.fold_in(jax.random.fold_in(own_key, 6), axis_at), (shards_of,), jnp.float32, smallest / len(shards), top_value / len(shards))
        factor_of = factor_of * jnp.repeat(jnp.exp(draws), extent[axis_at] // shards_of).reshape((-1,) + (1,) * (len(extent) - 1 - axis_at))
    return factor_of


def gaussian(key, dims, deviation, bound, pieces=(), held_as=jnp.bfloat16):
    level = block_levels(key, dims, pieces, -0.22, 0.18) if pieces else 1.0
    values = jax.random.normal(key, dims, jnp.float32) * deviation * level
    return jnp.minimum(jnp.maximum(values, -bound), bound).astype(held_as)


def setup_inputs(seed: int = 0) -> dict:
    key_list = jax.random.split(jax.random.key(seed), 7)
    pair_density = gaussian(key_list[0], (PAIRS, G), 1.0, 6.0, ((0, 4), (1, 8)))
    subspace = gaussian(key_list[1], (G, NB), G ** -0.5, 0.02734375, ((0, 8),))
    band_valence = draw_band_valence(jax.random.fold_in(key_list[6], 71), 0)
    band_conduction = draw_band_conduction(jax.random.fold_in(key_list[6], 71), 0)
    occupied = draw_occupied(jax.random.fold_in(key_list[6], 71), 0)
    energies = jnp.clip(jax.random.uniform(key_list[5], (NBANDS,), jnp.float32, -1.0, 1.0), -1.0, 1.0)
    return {"pair_density": pair_density, "subspace": subspace, "band_valence": band_valence, "band_conduction": band_conduction, "occupied": occupied, "energies": energies}


def pair_weights(band_valence, band_conduction, occupied, energies):
    energy_low = energies[band_valence]
    energy_high = energies[band_conduction]
    filled_low = occupied[band_valence].astype(jnp.float32)
    filled_high = occupied[band_conduction].astype(jnp.float32)
    scale = 1.0 / math.sqrt(PAIRS)
    return -2.0 * filled_low * (1.0 - filled_high) / (jnp.abs(energy_high - energy_low) + 0.5) * scale

def reference(pair_density, subspace, band_valence, band_conduction, occupied, energies):
    coefficient = jnp.dot(pair_density, subspace, preferred_element_type=jnp.float32)
    pair_weight = pair_weights(band_valence, band_conduction, occupied, energies)
    weighted = (coefficient * pair_weight[:, None]).astype(jnp.bfloat16)
    chi_panel = lax.dot_general(weighted, pair_density, (((0,), (0,)), ((), ())), preferred_element_type=jnp.float32)
    subspace_chi = lax.dot_general(subspace.astype(jnp.float32), chi_panel, (((0,), (1,)), ((), ())), precision=lax.Precision.HIGHEST)
    return (chi_panel, subspace_chi)
```

```python
import math

import jax
import jax.numpy as jnp
from jax import lax
from jax.experimental import pallas as pl
from jax.experimental.pallas import tpu as pltpu
from jax.sharding import PartitionSpec as P

VMEM = 18 << 20
COST = pl.CostEstimate(flops=1000, bytes_accessed=1000, transcendentals=0)


BLOCK = 384
WIDE = 768
CUTS = (1, 1, 1, 1)
TURNS = (2, 2, 2)
STEPS = 2


def split(extent, most):
    most = min(extent, most)
    return [(a, a + most) for a in range(0, extent, most)]


def split_bf16(value, pieces):
    out = []
    for _ in range(pieces):
        top = lax.reduce_precision(value, 8, 7)
        out.append(top.astype(jnp.bfloat16))
        value = value - top
    return out


def pair_weights(band_valence, band_conduction, occupied, energies, total_pairs):
    table = jnp.stack(split_bf16(energies, 3) + [occupied.astype(jnp.bfloat16)])
    levels = jnp.arange(energies.shape[0], dtype=jnp.int32)

    def lookup(indices):
        one_hot = (levels[:, None] == indices[None, :]).astype(jnp.bfloat16)
        rows = jnp.dot(table, one_hot, preferred_element_type=jnp.float32)
        return rows[0] + rows[1] + rows[2], rows[3]

    energy_low, filled_low = lookup(band_valence)
    energy_high, filled_high = lookup(band_conduction)
    scale = 1.0 / math.sqrt(total_pairs)
    return -2.0 * filled_low * (1.0 - filled_high) / (jnp.abs(energy_high - energy_low) + 0.5) * scale


def fitting(extent, most):
    for unit in (128, 1):
        for size in range(most // unit * unit, 0, -unit):
            if extent % size == 0:
                return size


def project(where, subspace, rho, start, stop, groups):
    depth, vectors = subspace.shape
    block = fitting(math.gcd(start, stop) if start else stop, BLOCK)

    def kernel(where_ref, s_ref, rho_ref, *refs):
        outs, found = refs[:-1], refs[-1]
        found[...] = jnp.dot(rho_ref[...], s_ref[...], preferred_element_type=jnp.float32).T
        first = where_ref[0] == 0

        def rows(part):
            got = [found[pl.ds(pl.multiple_of(where_ref[1 + n] + a, 8), b - a), :] for n, a, b in part]
            return jnp.concatenate(got) if len(got) > 1 else got[0]

        for at, (upper, lower) in enumerate(groups):
            upper, lower = rows(upper), rows(lower)
            outs[2 * at][...] = jnp.where(first, upper, lower)
            outs[2 * at + 1][...] = jnp.where(first, lower, upper)

    halves = [sum(b - a for _, a, b in group[0]) for group in groups for _ in (0, 1)]
    return pl.pallas_call(
        kernel,
        out_shape=[jax.ShapeDtypeStruct((h, stop - start), jnp.float32) for h in halves],
        grid_spec=pltpu.PrefetchScalarGridSpec(
            num_scalar_prefetch=1,
            grid=((stop - start) // block,),
            in_specs=[
                pl.BlockSpec(memory_space=pltpu.VMEM),
                pl.BlockSpec((block, depth), lambda i, at: (start // block + i, 0)),
            ],
            out_specs=[pl.BlockSpec((h, block), lambda i, at: (0, i)) for h in halves],
            scratch_shapes=[pltpu.VMEM((vectors, block), jnp.float32)],
        ),
        compiler_params=pltpu.CompilerParams(vmem_limit_bytes=VMEM),
        cost_estimate=COST,
    )(where, subspace, rho)


def panel(weighted, rho, step, steps, outputs, adds):
    rows, pairs = weighted.shape
    piece = rho.shape[1] // 2 // steps
    block = fitting(piece, WIDE)
    turns = piece // block

    def kernel(w_ref, rho_ref, *refs):
        more, outs = refs[: len(adds)], refs[len(adds) :]
        side, turn = pl.program_id(0), pl.program_id(1)
        found = jnp.dot(w_ref[...], rho_ref[...], preferred_element_type=jnp.float32)
        for s in (0, 1):

            @pl.when(side == s)
            def _():
                for at, ((a, b), sides) in enumerate(outputs):
                    if s not in sides:
                        continue
                    value = found[a:b]
                    for (output, its_side, _, _), ref in zip(adds, more):
                        if output == at and its_side == s:
                            value = value + ref[...]
                    outs[at][...] = value

    def of_output(sides):
        if len(sides) == 2:
            return lambda s, t: (0, s * turns + t)
        return (lambda s, t: (0, t + s * (turns - 1 - t))) if sides[0] == 0 else (lambda s, t: (0, s * t))

    def of_add(side, r):
        return (lambda s, t: (r, t + s * (turns - 1 - t))) if side == 0 else (lambda s, t: (r, s * t))

    return pl.pallas_call(
        kernel,
        out_shape=[
            jax.ShapeDtypeStruct((b - a, piece * len(sides)), jnp.float32) for (a, b), sides in outputs
        ],
        grid=(2, turns),
        in_specs=[
            pl.BlockSpec((rows, pairs), lambda s, t: (0, 0)),
            pl.BlockSpec((pairs, block), lambda s, t: (0, (step + s * steps) * turns + t)),
        ]
        + [
            pl.BlockSpec((outputs[at][0][1] - outputs[at][0][0], block), of_add(side, r))
            for at, side, _, r in adds
        ],
        out_specs=[pl.BlockSpec((b - a, block), of_output(sides)) for (a, b), sides in outputs],
        compiler_params=pltpu.CompilerParams(vmem_limit_bytes=VMEM),
        cost_estimate=COST,
    )(weighted, rho, *[a for _, _, a, _ in adds])


def assemble(chi, own, step, steps, low, high):
    rows, width = own.shape[0], own.shape[1] // 2 * 2 * steps
    piece = width // 2 // steps
    half = rows // 2
    arrived = low + high

    def kernel(*refs):
        own_ref, more, out_ref = refs[-2 - len(arrived)], refs[-1 - len(arrived) : -1], refs[-1]
        for part, got in ((slice(0, half), more[: len(low)]), (slice(half, rows), more[len(low) :])):
            value = own_ref[part, :]
            for ref in got:
                value = value + ref[...]
            out_ref[part, :] = value

    before = [] if chi is None else [chi]
    return pl.pallas_call(
        kernel,
        out_shape=jax.ShapeDtypeStruct((rows, width), own.dtype),
        grid=(2,),
        in_specs=[pl.BlockSpec(memory_space=pl.ANY)] * len(before)
        + [pl.BlockSpec((rows, piece), lambda s: (0, s))]
        + [pl.BlockSpec((half, piece), lambda s: (0, s))] * len(arrived),
        out_specs=pl.BlockSpec((rows, piece), lambda s: (0, step + s * steps)),
        input_output_aliases={0: 0} if before else {},
        compiler_params=pltpu.CompilerParams(vmem_limit_bytes=VMEM),
        cost_estimate=COST,
    )(*before, own, *arrived)


def body(rho, subspace, band_valence, band_conduction, occupied, energies):
    q, slabs = lax.axis_size("pair"), lax.axis_size("slab")
    pairs, width = rho.shape
    vectors = subspace.shape[1]
    rows = vectors // q
    inner = 2 if q % 2 == 0 else 1
    outer = q // inner
    chips = slabs // 2
    me, slab = lax.axis_index("pair"), lax.axis_index("slab")
    my_outer, my_inner = me // inner, me % inner
    core, chip = slab % 2, slab // 2
    last = []

    def run(work, *operands):
        n = len(operands)
        out = work(*lax.optimization_barrier((*operands, *last))[:n])
        last[:] = jax.tree.leaves(out)[:1]
        return out

    def target(offset):
        return (my_outer + offset[0]) % outer * inner + (my_inner + offset[1]) % inner

    def send_pair(x, offset):
        perm = [
            (s, (s // inner + offset[0]) % outer * inner + (s % inner + offset[1]) % inner)
            for s in range(q)
        ]
        return lax.ppermute(x, "pair", perm)

    def send_core(x):
        return lax.ppermute(x, "slab", [(s, s ^ 1) for s in range(slabs)])

    middle = chips // 2

    class Piece:
        def __init__(self, keep, send):
            self.total, self.hop, self.value = keep, -1, None
            self.got = send

        def receive(self):
            total, got, hop = self.total, self.got, self.hop
            if hop < 0:
                self.got = send_core(got)
            elif hop == 0:
                self.total = run(jnp.add, total, got)
            elif hop <= middle:
                here = (chip == hop) | (chip == chips - 1 - hop)
                if hop == middle:
                    here = (chip == middle - 1) | (chip == middle)
                self.total = run(lambda a, b: jnp.where(here, a + b, a), total, got)
            elif hop < 2 * middle:
                out = 2 * middle - hop
                here = (chip == out - 1) | (chip == chips - out)
                self.total = run(lambda a, b: jnp.where(here, b, a), total, got)
            else:
                self.value = (total, got)
            self.hop += 1

    def exchange(x, pairs, both=True):
        moves = pairs + [(b, a) for a, b in pairs] if both else pairs
        perm = [(2 * a + c, 2 * b + c) for a, b in moves for c in (0, 1)]
        if both:
            busy = {c for pair in pairs for c in pair}
            perm += [(2 * a + c, 2 * a + 1 - c) for a in range(chips) if a not in busy for c in (0, 1)]
        return lax.ppermute(x, "slab", perm)

    def advance(*groups):
        moving = [piece for group in groups for piece in group if piece.value is None]
        for piece in moving:
            piece.receive()
        for piece in moving:
            if piece.hop == 2 * middle and piece.value is None:
                piece.got = send_core(piece.total)
        for t in range(middle - 1, 0, -1):
            ins = [p for p in moving if p.hop == t]
            outs = [p for p in moving if p.hop == 2 * middle - t]
            pairs = [(t - 1, t), (chips - t, chips - 1 - t)]
            for back in outs:
                mate = next((p for p in ins if p.total.shape == back.total.shape), None)
                if mate is not None:
                    ins.remove(mate)
                    sender = (chip == t - 1) | (chip == chips - t)
                    both = run(lambda a, b: jnp.where(sender, a, b), mate.total, back.total)
                    back.got = mate.got = exchange(both, pairs)
                elif ins or any(p.hop < t for p in moving):
                    back.got = exchange(back.total, [(b, a) for a, b in pairs], False)
                else:
                    back.got = exchange(back.total, pairs)
            for piece in ins:
                piece.got = exchange(piece.total, pairs)
        for piece in moving:
            if piece.hop == middle:
                piece.got = exchange(piece.total, [(middle - 1, middle)])

    def finish(group, *others):
        while any(piece.value is None for piece in group):
            advance(group, *others)

    def cuts(sizes):
        unit, at, out = pairs // sum(sizes), 0, []
        for size in sizes:
            out.append((at, at + size * unit))
            at += size * unit
        return out

    mixed = [(y, x) for y in range(1, outer) for x in range(1, inner)]
    straight_x = [(0, x) for x in range(1, inner)]
    straight_y = [(y, 0) for y in range(1, outer)]
    straight = straight_x + straight_y
    own = [(0, 0)]
    n_mixed, half = len(mixed) * rows, rows // 2
    blocks = mixed + straight + own
    where = jnp.stack([core] + [target(o) * rows for o in blocks])

    def halves(group):
        left = sum(b - a for _, a, b in group) // 2
        upper, lower = [], []
        for offset, a, b in group:
            n, cut = blocks.index(offset), min(b, a + left)
            upper += [(n, a, cut)] if cut > a else []
            lower += [(n, cut, b)] if b > cut else []
            left -= cut - a
        return upper, lower

    groups = [
        halves([(o, 0, rows) for o in mixed]),
        halves([(o, 0, half) for o in straight]),
        halves([(o, half, rows) for o in straight]),
        halves([((0, 0), 0, rows)]),
    ]
    groups = [g for g in groups if g[0]]

    mixed_parts, found = [], []
    for cut in cuts(CUTS):
        out = run(lambda s: project(where, s, rho, *cut, groups), subspace)
        advance(mixed_parts)
        mixed_parts.append(Piece(*out[:2]))
        mixed_parts[-1].receive()
        found.append(out)

    def joined(at, turns):
        n = len(found) // turns
        return [
            [jnp.concatenate([f[2 * at + side] for f in found[k * n : (k + 1) * n]], 1) for side in (0, 1)]
            for k in range(turns)
        ]

    low_parts, high_parts, own_parts = [], [], []
    for at, group in enumerate((low_parts, high_parts, own_parts), 1):
        group += [Piece(*halves) for halves in joined(at, TURNS[at - 1])]

    weight = run(
        lambda *a: pair_weights(*a, pairs * q)[None, :], band_valence, band_conduction, occupied, energies
    )

    def gather(group):
        flat = [x for part in group for x in part.value]

        def work(*flat):
            halves = list(zip(flat[::2], flat[1::2]))
            upper = jnp.concatenate([jnp.where(core == 0, mine, other) for mine, other in halves], 1)
            lower = jnp.concatenate([jnp.where(core == 0, other, mine) for mine, other in halves], 1)
            sums = jnp.concatenate([upper, lower])
            return (sums * weight).astype(jnp.bfloat16), sums

        return run(work, *flat)

    steps = STEPS
    advance(mixed_parts)
    advance(mixed_parts, low_parts[:1])
    advance(mixed_parts, low_parts)
    advance(mixed_parts)
    advance(mixed_parts, low_parts)
    finish(mixed_parts)
    w_mixed, sum_mixed = gather(mixed_parts)

    def send_all(values, before):
        flat = run(lambda *v: v, *[v for v, _ in values], *before)
        return [send_pair(v, offset) for v, (_, offset) in zip(flat, values)]

    left, right = {}, {}
    before = []
    for k in range(steps):
        a, b = run(
            lambda w: panel(w, rho, k, steps, [((0, n_mixed), (0,)), ((0, n_mixed), (1,))], []), w_mixed
        )
        if k:
            advance(low_parts, high_parts)
        blocks = [slice(at * rows, (at + 1) * rows) for at in range(len(mixed))]
        got = send_all(
            [(a[block], (0, dx)) for block, (dy, dx) in zip(blocks, mixed)]
            + [(b[block], (dy, 0)) for block, (dy, dx) in zip(blocks, mixed)],
            before,
        )
        before = got
        for x, y, (dy, dx) in zip(got[: len(mixed)], got[len(mixed) :], mixed):
            left.setdefault((k, dy), []).append(x)
            right.setdefault((k, dx), []).append(y)
        if k == 0:
            advance(low_parts, high_parts[:1])
        else:
            advance(low_parts, high_parts, own_parts[:1])

    def straight_panel(w, k, part):
        adds = []
        for at, (dy, dx) in enumerate(straight):
            side, got = (0, left.get((k, dy))) if dy else (1, right.get((k, dx)))
            adds += [(at, side, x) for x in got or []]
        ends = [(at * half, (at + 1) * half) for at in range(len(straight))]

        def work(w, *extra):
            return panel(
                w, rho, k, steps, [(e, (0, 1)) for e in ends], [(o, s, x, part) for (o, s, _), x in zip(adds, extra)]
            )

        return run(work, w, *[x for _, _, x in adds])

    finish(low_parts)
    w_low, sum_low = gather(low_parts)
    low_arrived, high_arrived = [], []
    for k in range(steps):
        out = straight_panel(w_low, k, 0)
        if k:
            advance(high_parts, own_parts)
        before = send_all(list(zip(out, straight)), before)
        low_arrived.append(before)
        advance(high_parts, own_parts)

    finish(high_parts)
    w_high, sum_high = gather(high_parts)
    for k in range(steps):
        out = straight_panel(w_high, k, 1)
        if k:
            advance(own_parts)
        before = send_all(list(zip(out, straight)), before)
        high_arrived.append(before)
        advance(own_parts)

    finish(own_parts)
    w_own, sum_own = gather(own_parts)

    def by_block(mixed_rows, low_rows, high_rows, own_rows):
        blocks = {(0, 0): own_rows}
        for at, o in enumerate(mixed):
            blocks[o] = mixed_rows[at * rows : (at + 1) * rows]
        for at, o in enumerate(straight):
            block = slice(at * half, (at + 1) * half)
            blocks[o] = jnp.concatenate([low_rows[block], high_rows[block]])
        return jnp.concatenate([blocks[y, x] for y in range(outer) for x in range(inner)])

    def place(block):
        return (block // inner - my_outer) % outer * inner + (block % inner - my_inner) % inner

    slab_rows = vectors // slabs
    first_row = slab * slab_rows

    def local_sums(*parts):
        sums, weighted = by_block(*parts[:4]), by_block(*parts[4:])
        mine = lax.dynamic_slice_in_dim(
            sums, place(first_row // rows) * rows + first_row % rows, slab_rows
        )
        pieces = jnp.concatenate(split_bf16(mine, 2))
        local = lax.dot_general(
            pieces, weighted, (((1,), (1,)), ((), ())), preferred_element_type=jnp.float32
        )
        local = local[:slab_rows] + local[slab_rows:]
        return jnp.concatenate(
            [lax.dynamic_slice_in_dim(local, place(d) * rows, rows, 1) for d in range(q)], 1
        )

    local = run(local_sums, sum_mixed, sum_low, sum_high, sum_own, w_mixed, w_low, w_high, w_own)
    subspace_chi = lax.psum_scatter(local, "pair", scatter_dimension=1, tiled=True)

    own_sums = []
    for k in range(steps):
        own_sums += run(lambda w: panel(w, rho, k, steps, [((0, rows), (0, 1))], []), w_own)
    chi = None
    for k in range(steps):
        def work(own, *got, chi=chi):
            n = len(low_arrived[k])
            return assemble(chi, own, k, steps, list(got[:n]), list(got[n:]))

        chi = run(work, own_sums[k], *low_arrived[k], *high_arrived[k])
    return chi, subspace_chi


def solution(mesh):
    return jax.shard_map(
        body,
        mesh=mesh,
        in_specs=(P("pair", "slab"), P("slab", None), P("pair"), P("pair"), P(), P()),
        out_specs=(P("pair", "slab"), P("slab", "pair")),
        check_vma=False,
    )
```

```python
import math

import jax
import jax.numpy as jnp
from jax import lax
from jax.experimental import pallas as pl
from jax.experimental.pallas import tpu as pltpu
from jax.sharding import PartitionSpec as P

VMEM = 18 << 20
COST = pl.CostEstimate(flops=1000, bytes_accessed=1000, transcendentals=0)


BLOCK = 512
WIDE = 768
CUTS = (1, 1)
STEPS = 2


def split(extent, most):
    most = min(extent, most)
    return [(a, a + most) for a in range(0, extent, most)]


def split_bf16(value, pieces):
    out = []
    for _ in range(pieces):
        top = lax.reduce_precision(value, 8, 7)
        out.append(top.astype(jnp.bfloat16))
        value = value - top
    return out


def pair_weights(band_valence, band_conduction, occupied, energies, total_pairs):
    table = jnp.stack(split_bf16(energies, 3) + [occupied.astype(jnp.bfloat16)])
    levels = jnp.arange(energies.shape[0], dtype=jnp.int32)

    def lookup(indices):
        one_hot = (levels[:, None] == indices[None, :]).astype(jnp.bfloat16)
        rows = jnp.dot(table, one_hot, preferred_element_type=jnp.float32)
        return rows[0] + rows[1] + rows[2], rows[3]

    energy_low, filled_low = lookup(band_valence)
    energy_high, filled_high = lookup(band_conduction)
    scale = 1.0 / math.sqrt(total_pairs)
    return -2.0 * filled_low * (1.0 - filled_high) / (jnp.abs(energy_high - energy_low) + 0.5) * scale


def fitting(extent, most):
    for unit in (128, 1):
        for size in range(most // unit * unit, 0, -unit):
            if extent % size == 0:
                return size


def small(work, out_shapes, flags, *operands):
    def kernel(flags_ref, *refs):
        results = work(flags_ref, *[ref[...] for ref in refs[: len(operands)]])
        for ref, result in zip(refs[len(operands) :], results):
            ref[...] = result

    def whole(x):
        return pl.BlockSpec(x.shape, lambda i, flags: (0,) * len(x.shape))

    return pl.pallas_call(
        kernel,
        out_shape=out_shapes,
        grid_spec=pltpu.PrefetchScalarGridSpec(
            num_scalar_prefetch=1,
            grid=(1,),
            in_specs=[whole(x) for x in operands],
            out_specs=[whole(x) for x in out_shapes],
        ),
        compiler_params=pltpu.CompilerParams(vmem_limit_bytes=VMEM),
        cost_estimate=COST,
    )(flags, *operands)


def like(x):
    return jax.ShapeDtypeStruct(x.shape, x.dtype)


def project(where, subspace, rho, start, stop, groups):
    depth, vectors = subspace.shape
    block = fitting(math.gcd(start, stop) if start else stop, BLOCK)

    def kernel(where_ref, s_ref, rho_ref, *refs):
        outs, found = refs[:-1], refs[-1]
        found[...] = jnp.dot(rho_ref[...], s_ref[...], preferred_element_type=jnp.float32).T
        first = where_ref[0] == 0

        def rows(part):
            got = [found[pl.ds(pl.multiple_of(where_ref[1 + n] + a, 8), b - a), :] for n, a, b in part]
            return jnp.concatenate(got) if len(got) > 1 else got[0]

        for at, (upper, lower) in enumerate(groups):
            upper, lower = rows(upper), rows(lower)
            outs[2 * at][...] = jnp.where(first, upper, lower)
            outs[2 * at + 1][...] = jnp.where(first, lower, upper)

    halves = [sum(b - a for _, a, b in group[0]) for group in groups for _ in (0, 1)]
    return pl.pallas_call(
        kernel,
        out_shape=[jax.ShapeDtypeStruct((h, stop - start), jnp.float32) for h in halves],
        grid_spec=pltpu.PrefetchScalarGridSpec(
            num_scalar_prefetch=1,
            grid=((stop - start) // block,),
            in_specs=[
                pl.BlockSpec(memory_space=pltpu.VMEM),
                pl.BlockSpec((block, depth), lambda i, at: (start // block + i, 0)),
            ],
            out_specs=[pl.BlockSpec((h, block), lambda i, at: (0, i)) for h in halves],
            scratch_shapes=[pltpu.VMEM((vectors, block), jnp.float32)],
        ),
        compiler_params=pltpu.CompilerParams(vmem_limit_bytes=VMEM),
        cost_estimate=COST,
    )(where, subspace, rho)


def panel(weighted, rho, step, steps, outputs, adds):
    rows, pairs = weighted.shape
    piece = rho.shape[1] // 2 // steps
    block = fitting(piece, WIDE)
    turns = piece // block

    def kernel(w_ref, rho_ref, *refs):
        more, outs = refs[: len(adds)], refs[len(adds) :]
        side, turn = pl.program_id(0), pl.program_id(1)
        found = jnp.dot(w_ref[...], rho_ref[...], preferred_element_type=jnp.float32)
        for s in (0, 1):

            @pl.when(side == s)
            def _():
                for at, ((a, b), sides) in enumerate(outputs):
                    if s not in sides:
                        continue
                    value = found[a:b]
                    for (output, its_side, _, _), ref in zip(adds, more):
                        if output == at and its_side == s:
                            value = value + ref[...]
                    outs[at][...] = value

    def of_output(sides):
        if len(sides) == 2:
            return lambda s, t: (0, s * turns + t)
        return (lambda s, t: (0, t + s * (turns - 1 - t))) if sides[0] == 0 else (lambda s, t: (0, s * t))

    def of_add(side, r):
        return (lambda s, t: (r, t + s * (turns - 1 - t))) if side == 0 else (lambda s, t: (r, s * t))

    return pl.pallas_call(
        kernel,
        out_shape=[
            jax.ShapeDtypeStruct((b - a, piece * len(sides)), jnp.float32) for (a, b), sides in outputs
        ],
        grid=(2, turns),
        in_specs=[
            pl.BlockSpec((rows, pairs), lambda s, t: (0, 0)),
            pl.BlockSpec((pairs, block), lambda s, t: (0, (step + s * steps) * turns + t)),
        ]
        + [
            pl.BlockSpec((outputs[at][0][1] - outputs[at][0][0], block), of_add(side, r))
            for at, side, _, r in adds
        ],
        out_specs=[pl.BlockSpec((b - a, block), of_output(sides)) for (a, b), sides in outputs],
        compiler_params=pltpu.CompilerParams(vmem_limit_bytes=VMEM),
        cost_estimate=COST,
    )(weighted, rho, *[a for _, _, a, _ in adds])


def assemble(chi, own, step, steps, low, high):
    rows, width = own.shape[0], own.shape[1] // 2 * 2 * steps
    piece = width // 2 // steps
    half = rows // 2
    arrived = low + high

    def kernel(*refs):
        own_ref, more, out_ref = refs[-2 - len(arrived)], refs[-1 - len(arrived) : -1], refs[-1]
        for part, got in ((slice(0, half), more[: len(low)]), (slice(half, rows), more[len(low) :])):
            value = own_ref[part, :]
            for ref in got:
                value = value + ref[...]
            out_ref[part, :] = value

    before = [] if chi is None else [chi]
    return pl.pallas_call(
        kernel,
        out_shape=jax.ShapeDtypeStruct((rows, width), own.dtype),
        grid=(2,),
        in_specs=[pl.BlockSpec(memory_space=pl.ANY)] * len(before)
        + [pl.BlockSpec((rows, piece), lambda s: (0, s))]
        + [pl.BlockSpec((half, piece), lambda s: (0, s))] * len(arrived),
        out_specs=pl.BlockSpec((rows, piece), lambda s: (0, step + s * steps)),
        input_output_aliases={0: 0} if before else {},
        compiler_params=pltpu.CompilerParams(vmem_limit_bytes=VMEM),
        cost_estimate=COST,
    )(*before, own, *arrived)


def small_product(first, count, sums, weighted, stands):
    pairs = sums[0].shape[1]
    total = sum(x.shape[0] for x in sums)
    block = fitting(pairs, 512)
    n = len(sums)

    def kernel(first_ref, *refs):
        out, rows, others = refs[2 * n :]
        for group, to in ((refs[:n], rows), (refs[n : 2 * n], others)):
            for ref, at in zip(group, stands):
                size = ref.shape[0] // len(at)
                for k, start in enumerate(at):
                    to[pl.ds(start, size), :] = ref[pl.ds(k * size, size), :]
        mine = rows[pl.ds(pl.multiple_of(first_ref[0], 8), count), :]
        top = mine.astype(jnp.bfloat16)
        rest = (mine - top.astype(jnp.float32)).astype(jnp.bfloat16)
        dims = (((1,), (1,)), ((), ()))
        found = lax.dot_general(top, others[...], dims, preferred_element_type=jnp.float32)
        found = found + lax.dot_general(rest, others[...], dims, preferred_element_type=jnp.float32)

        @pl.when(pl.program_id(0) == 0)
        def _():
            out[...] = found

        @pl.when(pl.program_id(0) > 0)
        def _():
            out[...] += found

    return pl.pallas_call(
        kernel,
        out_shape=jax.ShapeDtypeStruct((count, total), jnp.float32),
        grid_spec=pltpu.PrefetchScalarGridSpec(
            num_scalar_prefetch=1,
            grid=(pairs // block,),
            in_specs=[pl.BlockSpec((x.shape[0], block), lambda i, at: (0, i)) for x in (*sums, *weighted)],
            out_specs=pl.BlockSpec((count, total), lambda i, at: (0, 0)),
            scratch_shapes=[pltpu.VMEM((total, block), jnp.float32), pltpu.VMEM((total, block), jnp.bfloat16)],
        ),
        compiler_params=pltpu.CompilerParams(vmem_limit_bytes=VMEM),
        cost_estimate=COST,
    )(first, *sums, *weighted)


def body(rho, subspace, band_valence, band_conduction, occupied, energies):
    q, slabs = lax.axis_size("pair"), lax.axis_size("slab")
    pairs, width = rho.shape
    vectors = subspace.shape[1]
    rows = vectors // q
    inner = 2 if q % 2 == 0 else 1
    outer = q // inner
    chips = slabs // 2
    me, slab = lax.axis_index("pair"), lax.axis_index("slab")
    my_outer, my_inner = me // inner, me % inner
    core, chip = slab % 2, slab // 2
    last = []

    def run(work, *operands):
        n = len(operands)
        out = work(*lax.optimization_barrier((*operands, *last))[:n])
        last[:] = jax.tree.leaves(out)
        return out

    def target(offset):
        return (my_outer + offset[0]) % outer * inner + (my_inner + offset[1]) % inner

    def send_pair(x, offset):
        perm = [
            (s, (s // inner + offset[0]) % outer * inner + (s % inner + offset[1]) % inner)
            for s in range(q)
        ]
        return lax.ppermute(x, "pair", perm)

    def send_core(x):
        return lax.ppermute(x, "slab", [(s, s ^ 1) for s in range(slabs)])

    middle = chips // 2

    class Piece:
        def __init__(self, keep, send):
            self.total, self.hop, self.value, self.moving = keep, 0, None, True
            self.got = send_core(send)

        def receive(self):
            if not self.moving:
                return
            total, got, hop = self.total, self.got, self.hop
            if hop == 0:
                self.total = run(jnp.add, total, got)
            elif hop <= middle:
                here = (chip == hop) | (chip == chips - 1 - hop)
                if hop == middle:
                    here = (chip == middle - 1) | (chip == middle)
                self.total = run(lambda a, b: jnp.where(here, a + b, a), total, got)
            else:
                out = 2 * middle - hop
                here = (chip == out - 1) | (chip == chips - out)
                self.total = run(lambda a, b: jnp.where(here, b, a), total, got)
            self.hop += 1
            self.moving = False

    def exchange(x, pairs, both=True):
        moves = pairs + [(b, a) for a, b in pairs] if both else pairs
        perm = [(2 * a + c, 2 * b + c) for a, b in moves for c in (0, 1)]
        if both:
            busy = {c for pair in pairs for c in pair}
            perm += [(2 * a + c, 2 * a + 1 - c) for a in range(chips) if a not in busy for c in (0, 1)]
        return lax.ppermute(x, "slab", perm)

    def advance(*groups):
        moving = [piece for group in groups for piece in group if piece.value is None]
        for piece in moving:
            piece.receive()
            piece.moving = piece.value is None
        for t in range(middle - 1, 0, -1):
            ins = [p for p in moving if p.hop == t]
            outs = [p for p in moving if p.hop == 2 * middle - t]
            pairs = [(t - 1, t), (chips - t, chips - 1 - t)]
            for back in outs:
                mate = next((p for p in ins if p.total.shape == back.total.shape), None)
                if mate is not None:
                    ins.remove(mate)
                    sender = (chip == t - 1) | (chip == chips - t)
                    both = run(lambda a, b: jnp.where(sender, a, b), mate.total, back.total)
                    back.got = mate.got = exchange(both, pairs)
                elif ins or any(p.hop < t for p in moving):
                    back.got = exchange(back.total, [(b, a) for a, b in pairs], False)
                else:
                    back.got = exchange(back.total, pairs)
            for piece in ins:
                piece.got = exchange(piece.total, pairs)
        for piece in moving:
            if piece.hop == middle:
                piece.got = exchange(piece.total, [(middle - 1, middle)])
        for piece in moving:
            if piece.hop == 2 * middle:
                piece.value = (piece.total, run(lambda x: x, send_core(piece.total)))
                piece.moving = False

    def finish(group, *others):
        while any(piece.value is None for piece in group):
            advance(group, *others)

    def cuts(sizes):
        unit, at, out = pairs // sum(sizes), 0, []
        for size in sizes:
            out.append((at, at + size * unit))
            at += size * unit
        return out

    mixed = [(y, x) for y in range(1, outer) for x in range(1, inner)]
    straight_x = [(0, x) for x in range(1, inner)]
    straight_y = [(y, 0) for y in range(1, outer)]
    straight = straight_x + straight_y
    own = [(0, 0)]
    n_mixed, half = len(mixed) * rows, rows // 2
    blocks = mixed + straight + own
    where = jnp.stack([core] + [target(o) * rows for o in blocks])

    def halves(group):
        left = sum(b - a for _, a, b in group) // 2
        upper, lower = [], []
        for offset, a, b in group:
            n, cut = blocks.index(offset), min(b, a + left)
            upper += [(n, a, cut)] if cut > a else []
            lower += [(n, cut, b)] if b > cut else []
            left -= cut - a
        return upper, lower

    groups = [
        halves([(o, 0, rows) for o in mixed]),
        halves([(o, 0, half) for o in straight]),
        halves([(o, half, rows) for o in straight]),
        halves([((0, 0), 0, rows)]),
    ]
    groups = [g for g in groups if g[0]]

    mixed_parts, low_parts, high_parts, own_parts = parts = [[] for _ in groups]

    def receive(*groups):
        for group in groups:
            for piece in group:
                piece.receive()

    for cut in cuts(CUTS):
        out = run(lambda s: project(where, s, rho, *cut, groups), subspace)
        halves_of = [out[2 * at : 2 * at + 2] for at in range(len(groups))]
        mixed_parts.append(Piece(*halves_of[0]))
        advance(mixed_parts[:-1])
        advance(mixed_parts[-1:])
        for group, both in zip(parts[1:], halves_of[1:]):
            group.append(Piece(*both))

    weight = run(
        lambda *a: pair_weights(*a, pairs * q)[None, :], band_valence, band_conduction, occupied, energies
    )

    def gather(group):
        flat = [x for part in group for x in part.value]

        half = flat[0].shape[0]

        def kernel(flags, weight, *flat):
            upper, lower = [], []
            for mine, other in zip(flat[::2], flat[1::2]):
                upper.append(jnp.where(flags[0] == 0, mine, other))
                lower.append(jnp.where(flags[0] == 0, other, mine))
            sums = jnp.concatenate([jnp.concatenate(upper, 1), jnp.concatenate(lower, 1)])
            return (sums * weight).astype(jnp.bfloat16), sums

        def work(*flat):
            shape = (2 * half, pairs)
            out = [jax.ShapeDtypeStruct(shape, jnp.bfloat16), jax.ShapeDtypeStruct(shape, jnp.float32)]
            return small(kernel, out, core[None], weight, *flat)

        return run(work, *flat)

    steps = STEPS
    receive(low_parts, high_parts, own_parts)
    advance(mixed_parts, low_parts[:1])
    advance(mixed_parts, low_parts)
    advance(mixed_parts, low_parts, high_parts[:1])
    finish(mixed_parts)
    w_mixed, sum_mixed = gather(mixed_parts)

    def send_all(values, before):
        flat = run(lambda *v: v, *[v for v, _ in values], *before)
        return [send_pair(v, offset) for v, (_, offset) in zip(flat, values)]

    left, right = {}, {}
    before = []
    for k in range(steps):
        a, b = run(
            lambda w: panel(w, rho, k, steps, [((0, n_mixed), (0,)), ((0, n_mixed), (1,))], []), w_mixed
        )
        if k:
            advance(low_parts, high_parts, own_parts[:1])
        blocks = [slice(at * rows, (at + 1) * rows) for at in range(len(mixed))]
        got = send_all(
            [(a[block], (0, dx)) for block, (dy, dx) in zip(blocks, mixed)]
            + [(b[block], (dy, 0)) for block, (dy, dx) in zip(blocks, mixed)],
            before,
        )
        before = got
        for x, y, (dy, dx) in zip(got[: len(mixed)], got[len(mixed) :], mixed):
            left.setdefault((k, dy), []).append(x)
            right.setdefault((k, dx), []).append(y)
        if k == 0:
            advance(low_parts, high_parts)

    def straight_panel(w, k, part):
        adds = []
        for at, (dy, dx) in enumerate(straight):
            side, got = (0, left.get((k, dy))) if dy else (1, right.get((k, dx)))
            adds += [(at, side, x) for x in got or []]
        ends = [(at * half, (at + 1) * half) for at in range(len(straight))]

        def work(w, *extra):
            return panel(
                w, rho, k, steps, [(e, (0, 1)) for e in ends], [(o, s, x, part) for (o, s, _), x in zip(adds, extra)]
            )

        return run(work, w, *[x for _, _, x in adds])

    finish(low_parts)
    w_low, sum_low = gather(low_parts)
    low_arrived, high_arrived = [], []
    for k in range(steps):
        out = straight_panel(w_low, k, 0)
        if k:
            advance(high_parts, own_parts)
        else:
            advance(high_parts, own_parts)
        before = send_all(list(zip(out, straight)), before)
        low_arrived.append(before)

    def rank(offset):
        return offset[0] * inner + offset[1]

    def place(block):
        return (block // inner - my_outer) % outer * inner + (block % inner - my_inner) % inner

    stands = [
        [rank(o) * rows for o in mixed],
        [rank(o) * rows for o in straight],
        [rank(o) * rows + half for o in straight],
        [0],
    ]
    slab_rows = vectors // slabs
    first_row = slab * slab_rows

    def local_sums(*groups):
        mine = place(first_row // rows) * rows + first_row % rows
        local = small_product(mine[None], slab_rows, groups[:4], groups[4:], stands)
        return [local[:, n * rows : (n + 1) * rows] for n in range(q)]

    finish(high_parts)
    w_high, sum_high = gather(high_parts)
    own_sums = []
    for k in range(steps):
        out = straight_panel(w_high, k, 1)
        if k == 0:
            advance(own_parts)
        else:
            finish(own_parts)
            w_own, sum_own = gather(own_parts)
            local = run(local_sums, sum_mixed, sum_low, sum_high, sum_own, w_mixed, w_low, w_high, w_own)
            arrivals = [send_pair(local[n], (n // inner, n % inner)) for n in range(1, q)]
            own_sums += run(lambda w: panel(w, rho, 0, steps, [((0, rows), (0, 1))], []), w_own)
        before = send_all(list(zip(out, straight)), before)
        high_arrived.append(before)

    for k in range(1, steps):
        own_sums += run(lambda w: panel(w, rho, k, steps, [((0, rows), (0, 1))], []), w_own)
    chi = None
    for k in range(steps):
        def work(own, *got, chi=chi):
            n = len(low_arrived[k])
            return assemble(chi, own, k, steps, list(got[:n]), list(got[n:]))

        chi = run(work, own_sums[k], *low_arrived[k], *high_arrived[k])
        if k == steps - 2:
            subspace_chi = run(lambda *x: sum(x[1:], x[0]), local[0], *arrivals)
    return chi, subspace_chi


def solution(mesh):
    return jax.shard_map(
        body,
        mesh=mesh,
        in_specs=(P("pair", "slab"), P("slab", None), P("pair"), P("pair"), P(), P()),
        out_specs=(P("pair", "slab"), P("slab", "pair")),
        check_vma=False,
    )
```

```python
import math

import jax
import jax.numpy as jnp
from jax import lax
from jax.experimental import pallas as pl
from jax.experimental.pallas import tpu as pltpu
from jax.sharding import PartitionSpec as P

VMEM = 26 << 20
COST = pl.CostEstimate(flops=1000, bytes_accessed=1000, transcendentals=0)


BLOCK = 512
CHUNKS = 4
WIDE = 1536
CUTS = (1, 1)
STEPS = 2


def split(extent, most):
    most = min(extent, most)
    return [(a, a + most) for a in range(0, extent, most)]


def split_bf16(value, pieces):
    out = []
    for _ in range(pieces):
        top = lax.reduce_precision(value, 8, 7)
        out.append(top.astype(jnp.bfloat16))
        value = value - top
    return out


def pair_weights(band_valence, band_conduction, occupied, energies, total_pairs):
    table = jnp.stack(split_bf16(energies, 3) + [occupied.astype(jnp.bfloat16)])
    levels = jnp.arange(energies.shape[0], dtype=jnp.int32)

    def lookup(indices):
        one_hot = (levels[:, None] == indices[None, :]).astype(jnp.bfloat16)
        rows = jnp.dot(table, one_hot, preferred_element_type=jnp.float32)
        return rows[0] + rows[1] + rows[2], rows[3]

    energy_low, filled_low = lookup(band_valence)
    energy_high, filled_high = lookup(band_conduction)
    scale = 1.0 / math.sqrt(total_pairs)
    return -2.0 * filled_low * (1.0 - filled_high) / (jnp.abs(energy_high - energy_low) + 0.5) * scale


def fitting(extent, most):
    for unit in (128, 1):
        for size in range(most // unit * unit, 0, -unit):
            if extent % size == 0:
                return size


def small(work, out_shapes, flags, *operands):
    def kernel(flags_ref, *refs):
        results = work(flags_ref, *[ref[...] for ref in refs[: len(operands)]])
        for ref, result in zip(refs[len(operands) :], results):
            ref[...] = result

    def whole(x):
        return pl.BlockSpec(x.shape, lambda i, flags: (0,) * len(x.shape))

    return pl.pallas_call(
        kernel,
        out_shape=out_shapes,
        grid_spec=pltpu.PrefetchScalarGridSpec(
            num_scalar_prefetch=1,
            grid=(1,),
            in_specs=[whole(x) for x in operands],
            out_specs=[whole(x) for x in out_shapes],
        ),
        compiler_params=pltpu.CompilerParams(vmem_limit_bytes=VMEM),
        cost_estimate=COST,
    )(flags, *operands)


def like(x):
    return jax.ShapeDtypeStruct(x.shape, x.dtype)


def project(where, subspace, rho, start, stop, groups):
    depth, vectors = subspace.shape
    block = fitting(math.gcd(start, stop) if start else stop, BLOCK)

    def kernel(where_ref, s_ref, rho_ref, *refs):
        outs, found = refs[:-1], refs[-1]
        found[...] = jnp.dot(rho_ref[...], s_ref[...], preferred_element_type=jnp.float32).T
        first = where_ref[0] == 0

        def rows(part):
            got = [found[pl.ds(pl.multiple_of(where_ref[1 + n] + a, 8), b - a), :] for n, a, b in part]
            return jnp.concatenate(got) if len(got) > 1 else got[0]

        for at, (upper, lower) in enumerate(groups):
            upper, lower = rows(upper), rows(lower)
            outs[2 * at][...] = jnp.where(first, upper, lower)
            outs[2 * at + 1][...] = jnp.where(first, lower, upper)

    halves = [sum(b - a for _, a, b in group[0]) for group in groups for _ in (0, 1)]
    return pl.pallas_call(
        kernel,
        out_shape=[jax.ShapeDtypeStruct((h, stop - start), jnp.float32) for h in halves],
        grid_spec=pltpu.PrefetchScalarGridSpec(
            num_scalar_prefetch=1,
            grid=((stop - start) // block,),
            in_specs=[
                pl.BlockSpec(memory_space=pltpu.VMEM),
                pl.BlockSpec((block, depth), lambda i, at: (start // block + i, 0)),
            ],
            out_specs=[pl.BlockSpec((h, block), lambda i, at: (0, i)) for h in halves],
            scratch_shapes=[pltpu.VMEM((vectors, block), jnp.float32)],
        ),
        compiler_params=pltpu.CompilerParams(vmem_limit_bytes=VMEM),
        cost_estimate=COST,
    )(where, subspace, rho)


def panel(weighted, rho, step, steps, outputs, adds, before=None):
    whole = before is not None
    before = before or []
    rows, pairs = weighted.shape
    piece = rho.shape[1] // 2 // steps
    block = fitting(piece, WIDE)
    turns = piece // block

    def kernel(w_ref, rho_ref, *refs):
        more, outs = refs[: len(adds)], refs[len(adds) + len(before) :]
        side, turn = pl.program_id(0), pl.program_id(1)
        found = jnp.dot(w_ref[...], rho_ref[...], preferred_element_type=jnp.float32)
        for s in (0, 1):

            @pl.when(side == s)
            def _():
                for at, ((a, b), sides) in enumerate(outputs):
                    if s not in sides:
                        continue
                    value = found[a:b]
                    for (output, its_side, _, _), ref in zip(adds, more):
                        if output == at and its_side == s:
                            value = value + ref[...]
                    outs[at][...] = value

    def of_output(sides):
        if len(sides) == 2:
            return lambda s, t: (0, ((step + s * steps) if whole else s) * turns + t)
        return (lambda s, t: (0, t + s * (turns - 1 - t))) if sides[0] == 0 else (lambda s, t: (0, s * t))

    def of_add(side, r):
        return (lambda s, t: (r, t + s * (turns - 1 - t))) if side == 0 else (lambda s, t: (r, s * t))

    return pl.pallas_call(
        kernel,
        out_shape=[
            jax.ShapeDtypeStruct((b - a, rho.shape[1] if whole else piece * len(sides)), jnp.float32)
            for (a, b), sides in outputs
        ],
        grid=(2, turns),
        in_specs=[
            pl.BlockSpec((rows, pairs), lambda s, t: (0, 0)),
            pl.BlockSpec((pairs, block), lambda s, t: (0, (step + s * steps) * turns + t)),
        ]
        + [
            pl.BlockSpec((outputs[at][0][1] - outputs[at][0][0], block), of_add(side, r))
            for at, side, _, r in adds
        ]
        + [pl.BlockSpec(memory_space=pl.ANY)] * len(before),
        input_output_aliases={2 + len(adds) + at: at for at in range(len(before))},
        out_specs=[pl.BlockSpec((b - a, block), of_output(sides)) for (a, b), sides in outputs],
        compiler_params=pltpu.CompilerParams(vmem_limit_bytes=VMEM),
        cost_estimate=COST,
    )(weighted, rho, *[a for _, _, a, _ in adds], *before)


def assemble(chi, own, step, steps, low, high):
    rows, width = own.shape[0], own.shape[1] // 2 * 2 * steps
    piece = width // 2 // steps
    half = rows // 2
    arrived = low + high

    def kernel(*refs):
        own_ref, more, out_ref = refs[-2 - len(arrived)], refs[-1 - len(arrived) : -1], refs[-1]
        for part, got in ((slice(0, half), more[: len(low)]), (slice(half, rows), more[len(low) :])):
            value = own_ref[part, :]
            for ref in got:
                value = value + ref[...]
            out_ref[part, :] = value

    before = [] if chi is None else [chi]
    return pl.pallas_call(
        kernel,
        out_shape=jax.ShapeDtypeStruct((rows, width), own.dtype),
        grid=(2,),
        in_specs=[pl.BlockSpec(memory_space=pl.ANY)] * len(before)
        + [pl.BlockSpec((rows, piece), lambda s: (0, s))]
        + [pl.BlockSpec((half, piece), lambda s: (0, s))] * len(arrived),
        out_specs=pl.BlockSpec((rows, piece), lambda s: (0, step + s * steps)),
        input_output_aliases={0: 0} if before else {},
        compiler_params=pltpu.CompilerParams(vmem_limit_bytes=VMEM),
        cost_estimate=COST,
    )(*before, own, *arrived)


def small_product(mine, weighted, stands):
    count, pairs = mine[0].shape
    total = sum(x.shape[0] for x in weighted)
    block = fitting(pairs, 512)
    n = len(mine)

    def kernel(*refs):
        out, others = refs[-2:]
        for ref, at in zip(refs[n:-2], stands):
            size = ref.shape[0] // len(at)
            for k, start in enumerate(at):
                others[pl.ds(start, size), :] = ref[pl.ds(k * size, size), :]
        rows = sum((ref[...] for ref in refs[1:n]), refs[0][...])
        top = rows.astype(jnp.bfloat16)
        rest = (rows - top.astype(jnp.float32)).astype(jnp.bfloat16)
        dims = (((1,), (1,)), ((), ()))
        found = lax.dot_general(top, others[...], dims, preferred_element_type=jnp.float32)
        found = found + lax.dot_general(rest, others[...], dims, preferred_element_type=jnp.float32)

        @pl.when(pl.program_id(0) == 0)
        def _():
            out[...] = found

        @pl.when(pl.program_id(0) > 0)
        def _():
            out[...] += found

    return pl.pallas_call(
        kernel,
        out_shape=jax.ShapeDtypeStruct((count, total), jnp.float32),
        grid=(pairs // block,),
        in_specs=[pl.BlockSpec((x.shape[0], block), lambda i: (0, i)) for x in (*mine, *weighted)],
        out_specs=pl.BlockSpec((count, total), lambda i: (0, 0)),
        scratch_shapes=[pltpu.VMEM((total, block), jnp.bfloat16)],
        compiler_params=pltpu.CompilerParams(vmem_limit_bytes=VMEM),
        cost_estimate=COST,
    )(*mine, *weighted)


def body(rho, subspace, band_valence, band_conduction, occupied, energies):
    q, slabs = lax.axis_size("pair"), lax.axis_size("slab")
    pairs, width = rho.shape
    vectors = subspace.shape[1]
    rows = vectors // q
    inner = 2 if q % 2 == 0 else 1
    outer = q // inner
    chips = slabs // 2
    me, slab = lax.axis_index("pair"), lax.axis_index("slab")
    my_outer, my_inner = me // inner, me % inner
    core, chip = slab % 2, slab // 2
    last = []

    def run(work, *operands):
        n = len(operands)
        out = work(*lax.optimization_barrier((*operands, *last))[:n])
        last[:] = jax.tree.leaves(out)
        return out

    def target(offset):
        return (my_outer + offset[0]) % outer * inner + (my_inner + offset[1]) % inner

    def send_pair(x, offset):
        perm = [
            (s, (s // inner + offset[0]) % outer * inner + (s % inner + offset[1]) % inner)
            for s in range(q)
        ]
        return lax.ppermute(x, "pair", perm)

    def send_core(x):
        return lax.ppermute(x, "slab", [(s, s ^ 1) for s in range(slabs)])

    middle = chips // 2

    class Piece:
        def __init__(self, keep, send):
            self.total, self.hop, self.value, self.moving = keep, 0, None, True
            self.got = send_core(send)

        def receive(self):
            if not self.moving:
                return
            total, got, hop = self.total, self.got, self.hop
            if hop == 0:
                self.total = run(jnp.add, total, got)
            elif hop <= middle:
                here = (chip == hop) | (chip == chips - 1 - hop)
                if hop == middle:
                    here = (chip == middle - 1) | (chip == middle)
                self.total = run(lambda a, b: jnp.where(here, a + b, a), total, got)
            else:
                out = 2 * middle - hop
                here = (chip == out - 1) | (chip == chips - out)
                self.total = run(lambda a, b: jnp.where(here, b, a), total, got)
            self.hop += 1
            self.moving = False

    def exchange(x, pairs, both=True):
        moves = pairs + [(b, a) for a, b in pairs] if both else pairs
        perm = [(2 * a + c, 2 * b + c) for a, b in moves for c in (0, 1)]
        if both:
            busy = {c for pair in pairs for c in pair}
            perm += [(2 * a + c, 2 * a + 1 - c) for a in range(chips) if a not in busy for c in (0, 1)]
        return lax.ppermute(x, "slab", perm)

    def advance(*groups):
        moving = [piece for group in groups for piece in group if piece.value is None]
        for piece in moving:
            piece.receive()
            piece.moving = piece.value is None
        for t in range(middle - 1, 0, -1):
            ins = [p for p in moving if p.hop == t]
            outs = [p for p in moving if p.hop == 2 * middle - t]
            pairs = [(t - 1, t), (chips - t, chips - 1 - t)]
            for back in outs:
                mate = next((p for p in ins if p.total.shape == back.total.shape), None)
                if mate is not None:
                    ins.remove(mate)
                    sender = (chip == t - 1) | (chip == chips - t)
                    both = run(lambda a, b: jnp.where(sender, a, b), mate.total, back.total)
                    back.got = mate.got = exchange(both, pairs)
                elif ins or any(p.hop < t for p in moving):
                    back.got = exchange(back.total, [(b, a) for a, b in pairs], False)
                else:
                    back.got = exchange(back.total, pairs)
            for piece in ins:
                piece.got = exchange(piece.total, pairs)
        for piece in moving:
            if piece.hop == middle:
                piece.got = exchange(piece.total, [(middle - 1, middle)])
        for piece in moving:
            if piece.hop == 2 * middle:
                piece.value = (piece.total, run(lambda x: x, send_core(piece.total)))
                piece.moving = False

    def finish(group, *others):
        while any(piece.value is None for piece in group):
            advance(group, *others)

    def cuts(sizes):
        unit, at, out = pairs // sum(sizes), 0, []
        for size in sizes:
            out.append((at, at + size * unit))
            at += size * unit
        return out

    mixed = [(y, x) for y in range(1, outer) for x in range(1, inner)]
    straight_x = [(0, x) for x in range(1, inner)]
    straight_y = [(y, 0) for y in range(1, outer)]
    straight = straight_x + straight_y
    own = [(0, 0)]
    n_mixed, half = len(mixed) * rows, rows // 2
    blocks = mixed + straight + own
    where = jnp.stack([core] + [target(o) * rows for o in blocks])

    def halves(group):
        left = sum(b - a for _, a, b in group) // 2
        upper, lower = [], []
        for offset, a, b in group:
            n, cut = blocks.index(offset), min(b, a + left)
            upper += [(n, a, cut)] if cut > a else []
            lower += [(n, cut, b)] if b > cut else []
            left -= cut - a
        return upper, lower

    groups = [
        halves([(o, 0, rows) for o in mixed]),
        halves([(o, 0, half) for o in straight]),
        halves([(o, half, rows) for o in straight]),
        halves([((0, 0), 0, rows)]),
    ]
    groups = [g for g in groups if g[0]]

    mixed_parts, low_parts, high_parts, own_parts = parts = [[] for _ in groups]

    def receive(*groups):
        for group in groups:
            for piece in group:
                piece.receive()

    for cut in cuts(CUTS):
        out = run(lambda s: project(where, s, rho, *cut, groups), subspace)
        halves_of = [out[2 * at : 2 * at + 2] for at in range(len(groups))]
        mixed_parts.append(Piece(*halves_of[0]))
        advance(mixed_parts[:-1])
        advance(mixed_parts[-1:])
        for group, both in zip(parts[1:], halves_of[1:]):
            group.append(Piece(*both))

    weight = run(
        lambda *a: pair_weights(*a, pairs * q)[None, :], band_valence, band_conduction, occupied, energies
    )

    def rank(offset):
        return offset[0] * inner + offset[1]

    def place(block):
        return (block // inner - my_outer) % outer * inner + (block % inner - my_inner) % inner

    stands = [
        [rank(o) * rows for o in mixed],
        [rank(o) * rows for o in straight],
        [rank(o) * rows + half for o in straight],
        [0],
    ]
    slab_rows = vectors // slabs
    first_row = slab * slab_rows
    mine = place(first_row // rows) * rows + first_row % rows

    def gather(group, stands):
        flat = [x for part in group for x in part.value]
        half_group = flat[0].shape[0]
        size = 2 * half_group // len(stands)
        starts = [a + b for a in stands for b in range(0, size, slab_rows)]

        def kernel(flags, weight, *flat):
            upper, lower = [], []
            for one, other in zip(flat[::2], flat[1::2]):
                upper.append(jnp.where(flags[0] == 0, one, other))
                lower.append(jnp.where(flags[0] == 0, other, one))
            sums = jnp.concatenate([jnp.concatenate(upper, 1), jnp.concatenate(lower, 1)])
            picked = jnp.zeros((slab_rows, pairs), jnp.float32)
            for n in range(len(starts)):
                rows_n = sums[n * slab_rows : (n + 1) * slab_rows]
                picked = jnp.where(flags[1 + n] != 0, rows_n, picked)
            return (sums * weight).astype(jnp.bfloat16), picked

        def work(*flat):
            out = [
                jax.ShapeDtypeStruct((2 * half_group, pairs), jnp.bfloat16),
                jax.ShapeDtypeStruct((slab_rows, pairs), jnp.float32),
            ]
            flags = jnp.stack([core] + [(mine == n).astype(jnp.int32) for n in starts])
            return small(kernel, out, flags, weight, *flat)

        return run(work, *flat)

    steps = STEPS
    receive(low_parts, high_parts, own_parts)
    advance(mixed_parts, low_parts[:1])
    advance(mixed_parts, low_parts)
    advance(mixed_parts, low_parts, high_parts[:1])
    finish(mixed_parts)
    w_mixed, sum_mixed = gather(mixed_parts, stands[0])

    def send_all(values, before):
        flat = run(lambda *v: v, *[v for v, _ in values], *before)
        return [send_pair(v, offset) for v, (_, offset) in zip(flat, values)]

    left, right = {}, {}
    before = []
    for k in range(steps):
        a, b = run(
            lambda w: panel(w, rho, k, steps, [((0, n_mixed), (0,)), ((0, n_mixed), (1,))], []), w_mixed
        )
        if k:
            advance(low_parts, high_parts, own_parts[:1])
        blocks = [slice(at * rows, (at + 1) * rows) for at in range(len(mixed))]
        got = send_all(
            [(a[block], (0, dx)) for block, (dy, dx) in zip(blocks, mixed)]
            + [(b[block], (dy, 0)) for block, (dy, dx) in zip(blocks, mixed)],
            before,
        )
        before = got
        for x, y, (dy, dx) in zip(got[: len(mixed)], got[len(mixed) :], mixed):
            left.setdefault((k, dy), []).append(x)
            right.setdefault((k, dx), []).append(y)
        if k == 0:
            advance(low_parts, high_parts)

    def straight_panel(w, k, part):
        adds = []
        for at, (dy, dx) in enumerate(straight):
            side, got = (0, left.get((k, dy))) if dy else (1, right.get((k, dx)))
            adds += [(at, side, x) for x in got or []]
        ends = [(at * half, (at + 1) * half) for at in range(len(straight))]

        extra = [x for _, _, x in adds]

        def work(w, *more):
            given = [(o, s, x, part) for (o, s, _), x in zip(adds, more)]
            return panel(w, rho, k, steps, [(e, (0, 1)) for e in ends], given)

        return run(work, w, *extra)

    finish(low_parts)
    w_low, sum_low = gather(low_parts, stands[1])
    low_arrived, high_arrived = [], []
    for k in range(steps):
        out = straight_panel(w_low, k, 0)
        advance(high_parts, own_parts)
        before = send_all(list(zip(out, straight)), before)
        low_arrived.append(before)

    finish(high_parts)
    w_high, sum_high = gather(high_parts, stands[2])
    own_sums = []

    def own_panel(k):
        return run(lambda w: panel(w, rho, k, steps, [((0, rows), (0, 1))], []), w_own)

    for k in range(steps):
        out = straight_panel(w_high, k, 1)
        if k == 0:
            advance(own_parts)
        else:
            finish(own_parts)
            w_own, sum_own = gather(own_parts, stands[3])
            own_sums += own_panel(0)
        before = send_all(list(zip(out, straight)), before)
        high_arrived.append(before)

    local = run(
        lambda *x: small_product(x[:4], x[4:], stands),
        *(sum_mixed, sum_low, sum_high, sum_own, w_mixed, w_low, w_high, w_own),
    )
    blocks = [local[:, n * rows : (n + 1) * rows] for n in range(q)]
    arrivals = [send_pair(blocks[n], (n // inner, n % inner)) for n in range(1, q)]
    for k in range(1, steps):
        own_sums += own_panel(k)
    chi = None
    for k in range(steps):

        def work(own, *got, chi=chi):
            n = len(low_arrived[k])
            return assemble(chi, own, k, steps, list(got[:n]), list(got[n:]))

        chi = run(work, own_sums[k], *low_arrived[k], *high_arrived[k])
        if k == steps - 2:
            subspace_chi = run(lambda *x: sum(x[1:], x[0]), blocks[0], *arrivals)
    return chi, subspace_chi


def solution(mesh):
    return jax.shard_map(
        body,
        mesh=mesh,
        in_specs=(P("pair", "slab"), P("slab", None), P("pair"), P("pair"), P(), P()),
        out_specs=(P("pair", "slab"), P("slab", "pair")),
        check_vma=False,
    )
```

```python
import math

import jax
import jax.numpy as jnp
from jax import lax
from jax.experimental import pallas as pl
from jax.experimental.pallas import tpu as pltpu
from jax.sharding import PartitionSpec as P

VMEM = 26 << 20
COST = pl.CostEstimate(flops=1000, bytes_accessed=1000, transcendentals=0)


BLOCK = 512
CHUNKS = 4
WIDE = 1536
CUTS = (1, 1)
STEPS = 2


def split(extent, most):
    most = min(extent, most)
    return [(a, a + most) for a in range(0, extent, most)]


def split_bf16(value, pieces):
    out = []
    for _ in range(pieces):
        top = lax.reduce_precision(value, 8, 7)
        out.append(top.astype(jnp.bfloat16))
        value = value - top
    return out


def pair_weights(band_valence, band_conduction, occupied, energies, total_pairs):
    table = jnp.stack(split_bf16(energies, 3) + [occupied.astype(jnp.bfloat16)])
    levels = jnp.arange(energies.shape[0], dtype=jnp.int32)

    def lookup(indices):
        one_hot = (levels[:, None] == indices[None, :]).astype(jnp.bfloat16)
        rows = jnp.dot(table, one_hot, preferred_element_type=jnp.float32)
        return rows[0] + rows[1] + rows[2], rows[3]

    energy_low, filled_low = lookup(band_valence)
    energy_high, filled_high = lookup(band_conduction)
    scale = 1.0 / math.sqrt(total_pairs)
    return -2.0 * filled_low * (1.0 - filled_high) / (jnp.abs(energy_high - energy_low) + 0.5) * scale


def fitting(extent, most):
    for unit in (128, 1):
        for size in range(most // unit * unit, 0, -unit):
            if extent % size == 0:
                return size


def small(work, out_shapes, flags, *operands):
    def kernel(flags_ref, *refs):
        results = work(flags_ref, *[ref[...] for ref in refs[: len(operands)]])
        for ref, result in zip(refs[len(operands) :], results):
            ref[...] = result

    def whole(x):
        return pl.BlockSpec(x.shape, lambda i, flags: (0,) * len(x.shape))

    return pl.pallas_call(
        kernel,
        out_shape=out_shapes,
        grid_spec=pltpu.PrefetchScalarGridSpec(
            num_scalar_prefetch=1,
            grid=(1,),
            in_specs=[whole(x) for x in operands],
            out_specs=[whole(x) for x in out_shapes],
        ),
        compiler_params=pltpu.CompilerParams(vmem_limit_bytes=VMEM),
        cost_estimate=COST,
    )(flags, *operands)


def like(x):
    return jax.ShapeDtypeStruct(x.shape, x.dtype)


def project(where, subspace, rho, start, stop, groups):
    depth, vectors = subspace.shape
    block = fitting(math.gcd(start, stop) if start else stop, BLOCK)

    def kernel(where_ref, s_ref, rho_ref, *refs):
        outs, found = refs[:-1], refs[-1]
        found[...] = jnp.dot(rho_ref[...], s_ref[...], preferred_element_type=jnp.float32).T
        first = where_ref[0] == 0

        def rows(part):
            got = [found[pl.ds(pl.multiple_of(where_ref[1 + n] + a, 8), b - a), :] for n, a, b in part]
            return jnp.concatenate(got) if len(got) > 1 else got[0]

        for at, (upper, lower) in enumerate(groups):
            upper, lower = rows(upper), rows(lower)
            outs[2 * at][...] = jnp.where(first, upper, lower)
            outs[2 * at + 1][...] = jnp.where(first, lower, upper)

    halves = [sum(b - a for _, a, b in group[0]) for group in groups for _ in (0, 1)]
    return pl.pallas_call(
        kernel,
        out_shape=[jax.ShapeDtypeStruct((h, stop - start), jnp.float32) for h in halves],
        grid_spec=pltpu.PrefetchScalarGridSpec(
            num_scalar_prefetch=1,
            grid=((stop - start) // block,),
            in_specs=[
                pl.BlockSpec(memory_space=pltpu.VMEM),
                pl.BlockSpec((block, depth), lambda i, at: (start // block + i, 0)),
            ],
            out_specs=[pl.BlockSpec((h, block), lambda i, at: (0, i)) for h in halves],
            scratch_shapes=[pltpu.VMEM((vectors, block), jnp.float32)],
        ),
        compiler_params=pltpu.CompilerParams(vmem_limit_bytes=VMEM),
        cost_estimate=COST,
    )(where, subspace, rho)


def panel(weighted, rho, step, steps, outputs, adds, before=None):
    whole = before is not None
    before = before or []
    rows, pairs = weighted.shape
    piece = rho.shape[1] // 2 // steps
    block = fitting(piece, WIDE)
    turns = piece // block

    def kernel(w_ref, rho_ref, *refs):
        more, outs = refs[: len(adds)], refs[len(adds) + len(before) :]
        side, turn = pl.program_id(0), pl.program_id(1)
        found = jnp.dot(w_ref[...], rho_ref[...], preferred_element_type=jnp.float32)
        for s in (0, 1):

            @pl.when(side == s)
            def _():
                for at, ((a, b), sides) in enumerate(outputs):
                    if s not in sides:
                        continue
                    value = found[a:b]
                    for (output, its_side, _, _), ref in zip(adds, more):
                        if output == at and its_side == s:
                            value = value + ref[...]
                    outs[at][...] = value

    def of_output(sides):
        if len(sides) == 2:
            return lambda s, t: (0, ((step + s * steps) if whole else s) * turns + t)
        return (lambda s, t: (0, t + s * (turns - 1 - t))) if sides[0] == 0 else (lambda s, t: (0, s * t))

    def of_add(side, r):
        return (lambda s, t: (r, t + s * (turns - 1 - t))) if side == 0 else (lambda s, t: (r, s * t))

    return pl.pallas_call(
        kernel,
        out_shape=[
            jax.ShapeDtypeStruct((b - a, rho.shape[1] if whole else piece * len(sides)), jnp.float32)
            for (a, b), sides in outputs
        ],
        grid=(2, turns),
        in_specs=[
            pl.BlockSpec((rows, pairs), lambda s, t: (0, 0)),
            pl.BlockSpec((pairs, block), lambda s, t: (0, (step + s * steps) * turns + t)),
        ]
        + [
            pl.BlockSpec((outputs[at][0][1] - outputs[at][0][0], block), of_add(side, r))
            for at, side, _, r in adds
        ]
        + [pl.BlockSpec(memory_space=pl.ANY)] * len(before),
        input_output_aliases={2 + len(adds) + at: at for at in range(len(before))},
        out_specs=[pl.BlockSpec((b - a, block), of_output(sides)) for (a, b), sides in outputs],
        compiler_params=pltpu.CompilerParams(vmem_limit_bytes=VMEM),
        cost_estimate=COST,
    )(weighted, rho, *[a for _, _, a, _ in adds], *before)


def assemble(chi, own, step, steps, low, high):
    rows, width = own.shape[0], own.shape[1] // 2 * 2 * steps
    piece = width // 2 // steps
    half = rows // 2
    arrived = low + high

    def kernel(*refs):
        own_ref, more, out_ref = refs[-2 - len(arrived)], refs[-1 - len(arrived) : -1], refs[-1]
        for part, got in ((slice(0, half), more[: len(low)]), (slice(half, rows), more[len(low) :])):
            value = own_ref[part, :]
            for ref in got:
                value = value + ref[...]
            out_ref[part, :] = value

    before = [] if chi is None else [chi]
    return pl.pallas_call(
        kernel,
        out_shape=jax.ShapeDtypeStruct((rows, width), own.dtype),
        grid=(2,),
        in_specs=[pl.BlockSpec(memory_space=pl.ANY)] * len(before)
        + [pl.BlockSpec((rows, piece), lambda s: (0, s))]
        + [pl.BlockSpec((half, piece), lambda s: (0, s))] * len(arrived),
        out_specs=pl.BlockSpec((rows, piece), lambda s: (0, step + s * steps)),
        input_output_aliases={0: 0} if before else {},
        compiler_params=pltpu.CompilerParams(vmem_limit_bytes=VMEM),
        cost_estimate=COST,
    )(*before, own, *arrived)


def small_product(mine, weighted, stands):
    count, pairs = mine[0].shape
    total = sum(x.shape[0] for x in weighted)
    block = fitting(pairs, 512)
    n = len(mine)

    def kernel(*refs):
        out, others = refs[-2:]
        for ref, at in zip(refs[n:-2], stands):
            size = ref.shape[0] // len(at)
            for k, start in enumerate(at):
                others[pl.ds(start, size), :] = ref[pl.ds(k * size, size), :]
        rows = sum((ref[...] for ref in refs[1:n]), refs[0][...])
        top = rows.astype(jnp.bfloat16)
        rest = (rows - top.astype(jnp.float32)).astype(jnp.bfloat16)
        dims = (((1,), (1,)), ((), ()))
        found = lax.dot_general(top, others[...], dims, preferred_element_type=jnp.float32)
        found = found + lax.dot_general(rest, others[...], dims, preferred_element_type=jnp.float32)

        @pl.when(pl.program_id(0) == 0)
        def _():
            out[...] = found

        @pl.when(pl.program_id(0) > 0)
        def _():
            out[...] += found

    return pl.pallas_call(
        kernel,
        out_shape=jax.ShapeDtypeStruct((count, total), jnp.float32),
        grid=(pairs // block,),
        in_specs=[pl.BlockSpec((x.shape[0], block), lambda i: (0, i)) for x in (*mine, *weighted)],
        out_specs=pl.BlockSpec((count, total), lambda i: (0, 0)),
        scratch_shapes=[pltpu.VMEM((total, block), jnp.bfloat16)],
        compiler_params=pltpu.CompilerParams(vmem_limit_bytes=VMEM),
        cost_estimate=COST,
    )(*mine, *weighted)


def body(rho, subspace, band_valence, band_conduction, occupied, energies):
    q, slabs = lax.axis_size("pair"), lax.axis_size("slab")
    pairs, width = rho.shape
    vectors = subspace.shape[1]
    rows = vectors // q
    inner = 2 if q % 2 == 0 else 1
    outer = q // inner
    chips = slabs // 2
    me, slab = lax.axis_index("pair"), lax.axis_index("slab")
    my_outer, my_inner = me // inner, me % inner
    core, chip = slab % 2, slab // 2
    last = []

    def run(work, *operands):
        n = len(operands)
        out = work(*lax.optimization_barrier((*operands, *last))[:n])
        last[:] = jax.tree.leaves(out)
        return out

    def target(offset):
        return (my_outer + offset[0]) % outer * inner + (my_inner + offset[1]) % inner

    def send_pair(x, offset):
        perm = [
            (s, (s // inner + offset[0]) % outer * inner + (s % inner + offset[1]) % inner)
            for s in range(q)
        ]
        return lax.ppermute(x, "pair", perm)

    def send_core(x):
        return lax.ppermute(x, "slab", [(s, s ^ 1) for s in range(slabs)])

    middle = chips // 2

    class Piece:
        def __init__(self, keep, send):
            self.total, self.hop, self.value, self.moving = keep, 0, None, True
            self.got = send_core(send)

        def receive(self):
            if not self.moving:
                return
            total, got, hop = self.total, self.got, self.hop
            if hop == 0:
                self.total = run(jnp.add, total, got)
            elif hop <= middle:
                here = (chip == hop) | (chip == chips - 1 - hop)
                if hop == middle:
                    here = (chip == middle - 1) | (chip == middle)
                self.total = run(lambda a, b: jnp.where(here, a + b, a), total, got)
            else:
                out = 2 * middle - hop
                here = (chip == out - 1) | (chip == chips - out)
                self.total = run(lambda a, b: jnp.where(here, b, a), total, got)
            self.hop += 1
            self.moving = False

    def exchange(x, pairs, both=True):
        moves = pairs + [(b, a) for a, b in pairs] if both else pairs
        perm = [(2 * a + c, 2 * b + c) for a, b in moves for c in (0, 1)]
        if both:
            busy = {c for pair in pairs for c in pair}
            perm += [(2 * a + c, 2 * a + 1 - c) for a in range(chips) if a not in busy for c in (0, 1)]
        return lax.ppermute(x, "slab", perm)

    def advance(*groups):
        moving = [piece for group in groups for piece in group if piece.value is None]
        for piece in moving:
            piece.receive()
            piece.moving = piece.value is None
        for t in range(middle - 1, 0, -1):
            ins = [p for p in moving if p.hop == t]
            outs = [p for p in moving if p.hop == 2 * middle - t]
            pairs = [(t - 1, t), (chips - t, chips - 1 - t)]
            for back in outs:
                mate = next((p for p in ins if p.total.shape == back.total.shape), None)
                if mate is not None:
                    ins.remove(mate)
                    sender = (chip == t - 1) | (chip == chips - t)
                    both = run(lambda a, b: jnp.where(sender, a, b), mate.total, back.total)
                    back.got = mate.got = exchange(both, pairs)
                elif ins or any(p.hop < t for p in moving):
                    back.got = exchange(back.total, [(b, a) for a, b in pairs], False)
                else:
                    back.got = exchange(back.total, pairs)
            for piece in ins:
                piece.got = exchange(piece.total, pairs)
        for piece in moving:
            if piece.hop == middle:
                piece.got = exchange(piece.total, [(middle - 1, middle)])
        for piece in moving:
            if piece.hop == 2 * middle:
                piece.value = (piece.total, run(lambda x: x, send_core(piece.total)))
                piece.moving = False

    def finish(group, *others):
        while any(piece.value is None for piece in group):
            advance(group, *others)

    def cuts(sizes):
        unit, at, out = pairs // sum(sizes), 0, []
        for size in sizes:
            out.append((at, at + size * unit))
            at += size * unit
        return out

    mixed = [(y, x) for y in range(1, outer) for x in range(1, inner)]
    straight_x = [(0, x) for x in range(1, inner)]
    straight_y = [(y, 0) for y in range(1, outer)]
    straight = straight_x + straight_y
    own = [(0, 0)]
    n_mixed, half = len(mixed) * rows, rows // 2
    blocks = mixed + straight + own
    where = jnp.stack([core] + [target(o) * rows for o in blocks])

    def halves(group):
        left = sum(b - a for _, a, b in group) // 2
        upper, lower = [], []
        for offset, a, b in group:
            n, cut = blocks.index(offset), min(b, a + left)
            upper += [(n, a, cut)] if cut > a else []
            lower += [(n, cut, b)] if b > cut else []
            left -= cut - a
        return upper, lower

    groups = [
        halves([(o, 0, rows) for o in mixed]),
        halves([(o, 0, half) for o in straight]),
        halves([(o, half, rows) for o in straight]),
        halves([((0, 0), 0, rows)]),
    ]
    groups = [g for g in groups if g[0]]

    mixed_parts, low_parts, high_parts, own_parts = parts = [[] for _ in groups]

    def receive(*groups):
        for group in groups:
            for piece in group:
                piece.receive()

    for cut in cuts(CUTS):
        out = run(lambda s: project(where, s, rho, *cut, groups), subspace)
        halves_of = [out[2 * at : 2 * at + 2] for at in range(len(groups))]
        mixed_parts.append(Piece(*halves_of[0]))
        advance(mixed_parts[:-1])
        advance(mixed_parts[-1:])
        for group, both in zip(parts[1:], halves_of[1:]):
            group.append(Piece(*both))

    weight = run(
        lambda *a: pair_weights(*a, pairs * q)[None, :], band_valence, band_conduction, occupied, energies
    )

    def rank(offset):
        return offset[0] * inner + offset[1]

    def place(block):
        return (block // inner - my_outer) % outer * inner + (block % inner - my_inner) % inner

    stands = [
        [rank(o) * rows for o in mixed],
        [rank(o) * rows for o in straight],
        [rank(o) * rows + half for o in straight],
        [0],
    ]
    slab_rows = vectors // slabs
    first_row = slab * slab_rows
    mine = place(first_row // rows) * rows + first_row % rows

    def gather(group, stands):
        flat = [x for part in group for x in part.value]
        half_group = flat[0].shape[0]
        size = 2 * half_group // len(stands)
        starts = [a + b for a in stands for b in range(0, size, slab_rows)]

        def kernel(flags, weight, *flat):
            upper, lower = [], []
            for one, other in zip(flat[::2], flat[1::2]):
                upper.append(jnp.where(flags[0] == 0, one, other))
                lower.append(jnp.where(flags[0] == 0, other, one))
            sums = jnp.concatenate([jnp.concatenate(upper, 1), jnp.concatenate(lower, 1)])
            picked = jnp.zeros((slab_rows, pairs), jnp.float32)
            for n in range(len(starts)):
                rows_n = sums[n * slab_rows : (n + 1) * slab_rows]
                picked = jnp.where(flags[1 + n] != 0, rows_n, picked)
            return (sums * weight).astype(jnp.bfloat16), picked

        def work(*flat):
            out = [
                jax.ShapeDtypeStruct((2 * half_group, pairs), jnp.bfloat16),
                jax.ShapeDtypeStruct((slab_rows, pairs), jnp.float32),
            ]
            flags = jnp.stack([core] + [(mine == n).astype(jnp.int32) for n in starts])
            return small(kernel, out, flags, weight, *flat)

        return run(work, *flat)

    steps = STEPS
    receive(low_parts, high_parts, own_parts)
    advance(mixed_parts, low_parts[:1])
    advance(mixed_parts, low_parts)
    advance(mixed_parts, low_parts, high_parts[:1])
    finish(mixed_parts)
    w_mixed, sum_mixed = gather(mixed_parts, stands[0])

    def send_all(values, before):
        flat = run(lambda *v: v, *[v for v, _ in values], *before)
        return [send_pair(v, offset) for v, (_, offset) in zip(flat, values)]

    left, right = {}, {}
    before = []
    for k in range(steps):
        a, b = run(
            lambda w: panel(w, rho, k, steps, [((0, n_mixed), (0,)), ((0, n_mixed), (1,))], []), w_mixed
        )
        if k:
            advance(low_parts, high_parts, own_parts[:1])
        blocks = [slice(at * rows, (at + 1) * rows) for at in range(len(mixed))]
        got = send_all(
            [(a[block], (0, dx)) for block, (dy, dx) in zip(blocks, mixed)]
            + [(b[block], (dy, 0)) for block, (dy, dx) in zip(blocks, mixed)],
            before,
        )
        before = got
        for x, y, (dy, dx) in zip(got[: len(mixed)], got[len(mixed) :], mixed):
            left.setdefault((k, dy), []).append(x)
            right.setdefault((k, dx), []).append(y)
        if k == 0:
            advance(low_parts, high_parts)

    def straight_panel(w, k, part):
        adds = []
        for at, (dy, dx) in enumerate(straight):
            side, got = (0, left.get((k, dy))) if dy else (1, right.get((k, dx)))
            adds += [(at, side, x) for x in got or []]
        ends = [(at * half, (at + 1) * half) for at in range(len(straight))]

        extra = [x for _, _, x in adds]

        def work(w, *more):
            given = [(o, s, x, part) for (o, s, _), x in zip(adds, more)]
            return panel(w, rho, k, steps, [(e, (0, 1)) for e in ends], given)

        return run(work, w, *extra)

    finish(low_parts)
    w_low, sum_low = gather(low_parts, stands[1])
    low_arrived, high_arrived = [], []
    for k in range(steps):
        out = straight_panel(w_low, k, 0)
        advance(high_parts, own_parts)
        before = send_all(list(zip(out, straight)), before)
        low_arrived.append(before)

    finish(high_parts)
    w_high, sum_high = gather(high_parts, stands[2])
    own_sums = []

    def own_panel(k):
        return run(lambda w: panel(w, rho, k, steps, [((0, rows), (0, 1))], []), w_own)

    for k in range(steps):
        out = straight_panel(w_high, k, 1)
        if k == 0:
            advance(own_parts)
        before = send_all(list(zip(out, straight)), before if k == 0 else low_arrived[-1])
        high_arrived.append(before)
    finish(own_parts)
    w_own, sum_own = gather(own_parts, stands[3])
    own_sums += own_panel(0)

    local = run(
        lambda *x: small_product(x[:4], x[4:], stands),
        *(sum_mixed, sum_low, sum_high, sum_own, w_mixed, w_low, w_high, w_own),
    )
    blocks = [local[:, n * rows : (n + 1) * rows] for n in range(q)]
    arrivals = [send_pair(blocks[n], (n // inner, n % inner)) for n in range(1, q)]
    for k in range(1, steps):
        own_sums += own_panel(k)
    chi = None
    for k in range(steps):

        def work(own, *got, chi=chi):
            n = len(low_arrived[k])
            return assemble(chi, own, k, steps, list(got[:n]), list(got[n:]))

        chi = run(work, own_sums[k], *low_arrived[k], *high_arrived[k])
        if k == steps - 2:
            subspace_chi = run(lambda *x: sum(x[1:], x[0]), blocks[0], *arrivals)
    return chi, subspace_chi


def solution(mesh):
    return jax.shard_map(
        body,
        mesh=mesh,
        in_specs=(P("pair", "slab"), P("slab", None), P("pair"), P("pair"), P(), P()),
        out_specs=(P("pair", "slab"), P("slab", "pair")),
        check_vma=False,
    )
```
